256 devices in a mesh: tm: 8 (over x, z_lo), chan: 32 (over z_hi, y, core).
Axes of the slice: x: 4, y: 4, z: 8 (z_hi: 4, z_lo: 2; z = z_hi * 2 + z_lo), core: 2. Of those that a mesh axis runs over, the one named last changes fastest.
Arguments:
- strain: bfloat16 [16384, 2048], P('tm', 'chan'), may hold values from -6 to 6
Outputs:
- covariances: float32 [16, 2048, 2048], P(None, 'chan', 'tm')
The draws below stay inside these ranges and needn't reach their ends.
All inputs are finite; a program needn't handle non-finite values.
Results may differ from the reference program's by a relative error of at most 0.0003.
Values may be sent and summed in bfloat16 or wider, within the bound.
No kernel may reach another device: no remote copies, remote signals or barrier semaphores. Data moves between devices by JAX's collectives and lax.ppermute only.
A program may use at most 64 MiB of HBM per device.

```python
import jax
import jax.numpy as jnp
from jax import lax

C = 2048
LAGS = 16
TOTAL = 16384


def with_spikes(result, rng, source, target, blocks, factor):
    owner, partner = [(jnp.arange(result.shape[dim]) // (result.shape[dim] // blocks)).reshape([-1 if axis == dim else 1 for axis in range(result.ndim)]) for dim in (source, target)]
    chosen = jax.random.permutation(rng, blocks)[partner]
    strong = (owner == chosen) | (owner == (partner + blocks // 2) % blocks)
    return jnp.where(strong, factor * result, result)


def shard_levels(own_key, shape, shards, low, top_value):
    factor_of, own = 1.0, jax.random.fold_in(own_key, 6)
    for axis_at, blocks in shards:
        steps = jnp.exp(jax.random.uniform(jax.random.fold_in(own, axis_at), (blocks,), jnp.float32, low / len(shards), top_value / len(shards)))
        factor_of = factor_of * jnp.repeat(steps, shape[axis_at] // blocks).reshape([-1 if axis == axis_at else 1 for axis in range(len(shape))])
    return factor_of


def bell_draw_with(stream_key, extent, spread, reach, split, heavy, dtype=jnp.bfloat16):
    values = spread * jax.random.normal(stream_key, extent, jnp.float32)
    if split:
        values = values * shard_levels(stream_key, extent, split, -0.22, 0.18)
    return jnp.clip(with_spikes(values, jax.random.fold_in(stream_key, 3), *heavy), -reach, reach).astype(dtype)


def setup_inputs(seed: int = 0) -> dict:
    keys = jax.random.split(jax.random.key(seed), 2)
    return {
        "strain": bell_draw_with(keys[0], (TOTAL, C), 1.0, 6.0, ((0, 8), (1, 32)), (0, 1, 32, 2.75)),
    }


def reference(strain):
    record = strain.astype(jnp.float32)
    blocks = []
    for lag in range(LAGS):
        later = record[lag:]
        earlier = record[:TOTAL - lag]
        summed = lax.dot_general(later, earlier, (((0,), (0,)), ((), ())), precision=lax.Precision.HIGHEST, preferred_element_type=jnp.float32)
        blocks.append(summed / jnp.float32(TOTAL - lag))
    return jnp.stack(blocks, axis=0)
```

```python
import jax
import jax.numpy as jnp
from jax import lax
from jax.experimental import pallas as pl
from jax.experimental.pallas import tpu as pltpu
from jax.sharding import Mesh, PartitionSpec as P

LAGS = 16
TOTAL = 16384
AXES = ("x", "zl", "zh", "y", "c")
SIZES = (4, 2, 4, 4, 2)
CH, SPAN, QUARTER, LANES = 128, 1024, 256, 128
OFFSETS = (0, 1, 3, 2)


def device_of(x, zl, zh, y, c):
    return (((x * 2 + zl) * 4 + zh) * 4 + y) * 2 + c


def scatter_pairs(quarter):
    pairs = []
    for x in range(4):
        for zl in range(2):
            for zh in range(4):
                for y in range(4):
                    to_zl = y // 2
                    to_y = y if zl == to_zl else (y + 2) % 4
                    for c in range(2):
                        target = device_of(zh, to_zl, (x + quarter) % 4, to_y, c)
                        pairs.append((device_of(x, zl, zh, y, c), target))
    return pairs


def pull(value, axis, offset, count):
    return lax.ppermute(value, axis, [((i + offset) % count, i) for i in range(count)])


def swap(value, axis, bits, count):
    return lax.ppermute(value, axis, [(i, i ^ bits) for i in range(count)])


def kernel(ix, rows_0, rows_1, rows_3, rows_2, *refs):
    cols, (keep, send, rows, later, earlier, total) = refs[:16], refs[16:]
    x, zl, zh, y, c = (ix[i] for i in range(5))
    for offset, slabs in zip(OFFSETS, (rows_0, rows_1, rows_3, rows_2)):
        for m in range(2):
            rows[lax.rem(x + offset, 4), lax.rem(zl + m, 2)] = slabs[m]
    half = lax.rem(y, 2)
    zl_own = lax.select(lax.div(y, 2) == zl, zl, 1 - zl)
    for at, offset in enumerate(OFFSETS):
        for pair in range(2):
            zl_slab = zl_own if pair == 0 else 1 - zl_own
            for q in range(4):
                x_slab = lax.rem(zh + offset - q + 8, 4)
                window = rows[x_slab, zl_slab, :, pl.ds(QUARTER * q, QUARTER + LANES)]
                for lag in range(LAGS):
                    later[lag * CH : (lag + 1) * CH, QUARTER * q : QUARTER * (q + 1)] = window[:, lag : lag + QUARTER]
            same, other = cols[4 * at + 2 * pair : 4 * at + 2 * pair + 2]
            earlier[pl.ds(pl.multiple_of(half * CH, CH), CH), :] = same[...]
            earlier[pl.ds(pl.multiple_of((1 - half) * CH, CH), CH), :] = other[...]
            part = lax.dot_general(
                later[...], earlier[...], (((1,), (1,)), ((), ())), preferred_element_type=jnp.float32
            )
            if at == 0 and pair == 0:
                total[...] = part
            else:
                total[...] += part
    for lag in range(LAGS):
        keep[lag] = total[pl.ds(pl.multiple_of(lag * CH + c * 64, 64), 64), :]
        send[lag] = total[pl.ds(pl.multiple_of(lag * CH + (1 - c) * 64, 64), 64), :]


def products(ix, rows, cols):
    vmem = pl.BlockSpec(memory_space=pltpu.VMEM)
    half = jax.ShapeDtypeStruct((LAGS, 64, 256), jnp.float32)
    return pl.pallas_call(
        kernel,
        out_shape=(half, half),
        in_specs=[pl.BlockSpec(memory_space=pltpu.SMEM)] + [vmem] * 20,
        out_specs=(vmem, vmem),
        scratch_shapes=[
            pltpu.VMEM((4, 2, CH, SPAN + LANES), jnp.bfloat16),
            pltpu.VMEM((LAGS * CH, SPAN), jnp.bfloat16),
            pltpu.VMEM((256, SPAN), jnp.bfloat16),
            pltpu.VMEM((LAGS * CH, 256), jnp.float32),
        ],
        compiler_params=pltpu.CompilerParams(vmem_limit_bytes=48 * 2**20),
        cost_estimate=pl.CostEstimate(flops=2 * 2048 * 256 * 8192, bytes_accessed=8 * 2**20, transcendentals=0),
    )(ix, *rows, *cols)


def spread(one, two):
    one_1, two_1 = swap(one, "y", 1, 4), swap(two, "y", 1, 4)
    one_3, two_3 = swap(one, "y", 3, 4), swap(two, "y", 3, 4)
    one_2, two_2 = swap(one_1, "y", 3, 4), swap(two_3, "y", 1, 4)
    return [one, one_1, one_2, one_3], [two, two_1, two_2, two_3]


def on_device(strain):
    c = lax.axis_index("c")
    own = strain.T
    mine = lax.dynamic_slice(own, (0, c * SPAN), (64, SPAN))
    others = lax.dynamic_slice(own, (0, (1 - c) * SPAN), (64, SPAN))
    got = swap(others, "c", 1, 2)
    block = jnp.where(c == 0, jnp.concatenate([mine, got]), jnp.concatenate([got, mine]))

    quarters = [
        lax.ppermute(block[:, QUARTER * q : QUARTER * (q + 1)], AXES, scatter_pairs(q)) for q in range(4)
    ]
    held = jnp.concatenate(quarters, axis=1)

    head = lax.ppermute(block[:, :LANES], ("x", "zl", "c"), [(i, i - 1) for i in range(1, 16)])
    slab = jnp.concatenate([block, head], axis=1)
    slabs = jnp.stack([slab, swap(slab, "zl", 1, 2)])
    rows = [slabs] + [pull(slabs, "x", offset, 4) for offset in OFFSETS[1:]]

    above, below = pull(held, "zh", 1, 4), pull(held, "zh", 3, 4)
    across = pull(held, "zh", 2, 4)
    cols_1, cols_3 = spread(above, below)
    cols_0, cols_2 = spread(held, across)

    ix = jnp.stack([lax.axis_index(name) for name in AXES]).astype(jnp.int32)
    order = [c4[i] for c4 in (cols_0, cols_1, cols_3, cols_2) for i in (0, 1, 2, 3)]
    keep, send = products(ix, rows, order)
    summed = keep + swap(send, "c", 1, 2)
    counts = jnp.float32(TOTAL) - jnp.arange(LAGS, dtype=jnp.float32)
    return summed / counts[:, None, None]


def solution(mesh):
    fine = Mesh(mesh.devices.reshape(SIZES), AXES)
    return jax.shard_map(
        on_device,
        mesh=fine,
        in_specs=(P(("x", "zl"), ("zh", "y", "c")),),
        out_specs=P(None, ("zh", "y", "c"), ("x", "zl")),
        check_vma=False,
    )
```

```python
import jax
import jax.numpy as jnp
from jax import lax
from jax.experimental import pallas as pl
from jax.experimental.pallas import tpu as pltpu
from jax.sharding import Mesh, PartitionSpec as P

LAGS = 16
TOTAL = 16384
AXES = ("x", "zl", "zh", "y", "c")
SIZES = (4, 2, 4, 4, 2)
CH, SPAN, QUARTER, LANES = 128, 1024, 256, 128
OFFSETS = (0, 1, 3, 2)


def device_of(x, zl, zh, y, c):
    return (((x * 2 + zl) * 4 + zh) * 4 + y) * 2 + c


def scatter_pairs(quarter):
    pairs = []
    for x in range(4):
        for zl in range(2):
            for zh in range(4):
                for y in range(4):
                    to_zl = y // 2
                    to_y = y if zl == to_zl else (y + 2) % 4
                    for c in range(2):
                        target = device_of(zh, to_zl, (x + quarter) % 4, to_y, c)
                        pairs.append((device_of(x, zl, zh, y, c), target))
    return pairs


def pull(value, axis, offset, count):
    return lax.ppermute(value, axis, [((i + offset) % count, i) for i in range(count)])


def swap(value, axis, bits, count):
    return lax.ppermute(value, axis, [(i, i ^ bits) for i in range(count)])


def make_kernel(pieces, first, last):
    def kernel(ix, rows, *refs):
        refs = list(refs)
        cols = [refs.pop(0) for _ in range(2 * len(pieces))]
        before = None if first else refs.pop(0)
        outs = [refs.pop(0) for _ in range(2 if last else 1)]
        windows, earlier, later, sems = refs[:4]
        total = refs[4] if last else outs[0]
        zl, zh, y, c = (ix[i] for i in range(1, 5))
        half = lax.rem(y, 2)
        zl_own = lax.select(lax.div(y, 2) == zl, zl, 1 - zl)
        copies = []
        for i, (offset, pair) in enumerate(pieces):
            zl_slab = zl_own if pair == 0 else 1 - zl_own
            mine = []
            for q in range(4):
                slab = lax.rem(zh + offset - q + 8, 4) * 2 + zl_slab
                source = rows.at[slab, :, pl.ds(QUARTER * q, QUARTER + LANES)]
                mine.append(pltpu.make_async_copy(source, windows.at[i, q], sems.at[i, q]))
            for j, place in enumerate((half, 1 - half)):
                target = earlier.at[i, pl.ds(pl.multiple_of(place * CH, CH), CH), :]
                mine.append(pltpu.make_async_copy(cols[2 * i + j], target, sems.at[i, 4 + j]))
            for copy in mine:
                copy.start()
            copies.append(mine)
        for i in range(len(pieces)):
            for copy in copies[i]:
                copy.wait()
            for q in range(4):
                window = windows[i, q]
                for lag in range(LAGS):
                    later[lag * CH : (lag + 1) * CH, QUARTER * q : QUARTER * (q + 1)] = window[:, lag : lag + QUARTER]
            for s in range(4):
                span = slice(512 * s, 512 * (s + 1))
                part = lax.dot_general(
                    later[span, :], earlier[i], (((1,), (1,)), ((), ())), preferred_element_type=jnp.float32
                )
                if i > 0:
                    total[span, :] += part
                elif first:
                    total[span, :] = part
                else:
                    total[span, :] = before[span, :] + part
        if last:
            keep, send = outs
            for lag in range(LAGS):
                scale = jnp.float32(1.0 / (TOTAL - lag))
                keep[lag] = total[pl.ds(pl.multiple_of(lag * CH + c * 64, 64), 64), :] * scale
                send[lag] = total[pl.ds(pl.multiple_of(lag * CH + (1 - c) * 64, 64), 64), :] * scale

    return kernel


def products(ix, rows, pieces, before=None, last=False):
    vmem, anywhere = pl.BlockSpec(memory_space=pltpu.VMEM), pl.BlockSpec(memory_space=pl.ANY)
    n, first = len(pieces), before is None
    sums = jax.ShapeDtypeStruct((LAGS * CH, 256), jnp.float32)
    half = jax.ShapeDtypeStruct((LAGS, 64, 256), jnp.float32)
    scratch = [
        pltpu.VMEM((n, 4, CH, QUARTER + LANES), jnp.bfloat16),
        pltpu.VMEM((n, 256, SPAN), jnp.bfloat16),
        pltpu.VMEM((LAGS * CH, SPAN), jnp.bfloat16),
        pltpu.SemaphoreType.DMA((n, 6)),
    ]
    return pl.pallas_call(
        make_kernel([piece[:2] for piece in pieces], first, last),
        out_shape=(half, half) if last else sums,
        in_specs=[pl.BlockSpec(memory_space=pltpu.SMEM)] + [anywhere] * (1 + 2 * n) + ([] if first else [vmem]),
        out_specs=(vmem, vmem) if last else vmem,
        scratch_shapes=scratch + ([pltpu.VMEM((LAGS * CH, 256), jnp.float32)] if last else []),
        input_output_aliases={} if first or last else {2 + 2 * n: 0},
        compiler_params=pltpu.CompilerParams(vmem_limit_bytes=28 * 2**20),
        cost_estimate=pl.CostEstimate(flops=n * 2 * 2048 * 256 * 1024, bytes_accessed=n * 2**20, transcendentals=0),
    )(ix, rows, *[block for piece in pieces for block in piece[2:]], *([] if first else [before]))


def spread(one, two):
    one_1, two_1 = swap(one, "y", 1, 4), swap(two, "y", 1, 4)
    one_3, two_3 = swap(one, "y", 3, 4), swap(two, "y", 3, 4)
    one_2, two_2 = swap(one_1, "y", 3, 4), swap(two_3, "y", 1, 4)
    return [one, one_1, one_2, one_3], [two, two_1, two_2, two_3]


def on_device(strain):
    c = lax.axis_index("c")
    own = strain.T
    mine = lax.dynamic_slice(own, (0, c * SPAN), (64, SPAN))
    others = lax.dynamic_slice(own, (0, (1 - c) * SPAN), (64, SPAN))
    got = swap(others, "c", 1, 2)
    block = jnp.where(c == 0, jnp.concatenate([mine, got]), jnp.concatenate([got, mine]))

    quarters = [
        lax.ppermute(block[:, QUARTER * q : QUARTER * (q + 1)], AXES, scatter_pairs(q)) for q in range(4)
    ]
    held = jnp.concatenate(quarters, axis=1)

    head = lax.ppermute(block[:, :LANES], ("x", "zl", "c"), [(i, i - 1) for i in range(1, 16)])
    slab = jnp.concatenate([block, head], axis=1)
    rows = lax.all_to_all(
        jnp.broadcast_to(slab[None], (8, CH, SPAN + LANES)), ("x", "zl"), 0, 0, tiled=True
    )

    above, below = pull(held, "zh", 1, 4), pull(held, "zh", 3, 4)
    across = pull(held, "zh", 2, 4)
    cols_1, cols_3 = spread(above, below)
    cols_0, cols_2 = spread(held, across)

    ix = jnp.stack([lax.axis_index(name) for name in AXES]).astype(jnp.int32)
    sums = products(ix, rows, [(0, 0, *cols_0[:2]), (0, 1, *cols_0[2:])])
    sums = products(ix, rows, [(1, 0, *cols_1[:2]), (3, 0, *cols_3[:2])], sums)
    sums = products(ix, rows, [(1, 1, *cols_1[2:]), (3, 1, *cols_3[2:])], sums)
    sums = products(ix, rows, [(2, 0, *cols_2[:2])], sums)
    keep, send = products(ix, rows, [(2, 1, *cols_2[2:])], sums, last=True)
    return keep + swap(send, "c", 1, 2)


def solution(mesh):
    fine = Mesh(mesh.devices.reshape(SIZES), AXES)
    return jax.shard_map(
        on_device,
        mesh=fine,
        in_specs=(P(("x", "zl"), ("zh", "y", "c")),),
        out_specs=P(None, ("zh", "y", "c"), ("x", "zl")),
        check_vma=False,
    )
```

```python
import jax
import jax.numpy as jnp
from jax import lax
from jax.experimental import pallas as pl
from jax.experimental.pallas import tpu as pltpu
from jax.sharding import Mesh, PartitionSpec as P

LAGS = 16
TOTAL = 16384
AXES = ("x", "zl", "zh", "y", "c")
SIZES = (4, 2, 4, 4, 2)
CH, SPAN, QUARTER, LANES = 128, 1024, 256, 128
OFFSETS = (0, 1, 3, 2)
ROWS_AT = (0, 1, 3, 2)
VLIM = 28


def device_of(x, zl, zh, y, c):
    return (((x * 2 + zl) * 4 + zh) * 4 + y) * 2 + c


def scatter_pairs(quarter):
    pairs = []
    for x in range(4):
        for zl in range(2):
            for zh in range(4):
                for y in range(4):
                    to_zl = y // 2
                    to_y = y if zl == to_zl else (y + 2) % 4
                    for c in range(2):
                        target = device_of(zh, to_zl, (x + quarter) % 4, to_y, c)
                        pairs.append((device_of(x, zl, zh, y, c), target))
    return pairs


def pull(value, axis, offset, count):
    return lax.ppermute(value, axis, [((i + offset) % count, i) for i in range(count)])


def swap(value, axis, bits, count):
    return lax.ppermute(value, axis, [(i, i ^ bits) for i in range(count)])


def make_kernel(pieces, n_arrays, first, last):
    n = len(pieces)

    def kernel(ix, *refs):
        refs = list(refs)
        rows = [refs.pop(0) for _ in OFFSETS]
        arrays = [refs.pop(0) for _ in range(n_arrays)]
        before = None if first else refs.pop(0)
        outs = [refs.pop(0) for _ in range(2 if last else 1)]
        windows, earlier, sems = refs[:3]
        total = refs[3] if last else outs[0]
        x, zl, zh, y, c = (ix[i] for i in range(5))
        half = lax.rem(y, 2)
        away_zl = lax.select(lax.div(y, 2) == zl, 0, 1)
        copies = []
        for i, (offset, pair, blocks) in enumerate(pieces):
            m = away_zl if pair == 0 else 1 - away_zl
            mine = []
            for q in range(4):
                away = lax.rem(zh + offset - q - x + 8, 4)
                for at, slabs in zip(ROWS_AT, rows):
                    source = slabs.at[m, :, pl.ds(QUARTER * q, QUARTER + LANES)]
                    copy = pltpu.make_async_copy(source, windows.at[i, q], sems.at[i, q])
                    pl.when(away == at)(copy.start)
                mine.append(copy)
            for j, (parts, place) in enumerate(zip(blocks, (half, 1 - half))):
                size = CH // len(parts)
                for s, (number, index) in enumerate(parts):
                    start = pl.multiple_of(place * CH + s * size, size)
                    source = arrays[number] if index is None else arrays[number].at[index]
                    copy = pltpu.make_async_copy(source, earlier.at[i, pl.ds(start, size), :], sems.at[i, 4 + 2 * j + s])
                    copy.start()
                    mine.append(copy)
            copies.append(mine)
        for i in range(n):
            for copy in copies[i]:
                copy.wait()
            wide = [windows[i, q] for q in range(4)]
            for s in range(4):
                span = slice(512 * s, 512 * (s + 1))
                later = jnp.concatenate(
                    [
                        jnp.concatenate([window[:, lag : lag + QUARTER] for window in wide], axis=1)
                        for lag in range(4 * s, 4 * s + 4)
                    ],
                    axis=0,
                )
                part = lax.dot_general(
                    later, earlier[i], (((1,), (1,)), ((), ())), preferred_element_type=jnp.float32
                )
                if i > 0:
                    total[span, :] += part
                elif first:
                    total[span, :] = part
                else:
                    total[span, :] = before[span, :] + part
        if last:
            keep, send = outs
            for lag in range(LAGS):
                scale = jnp.float32(1.0 / (TOTAL - lag))
                keep[lag] = total[pl.ds(pl.multiple_of(lag * CH + c * 64, 64), 64), :] * scale
                send[lag] = total[pl.ds(pl.multiple_of(lag * CH + (1 - c) * 64, 64), 64), :] * scale

    return kernel


def products(ix, rows, pieces, before=None, last=False):
    vmem, anywhere = pl.BlockSpec(memory_space=pltpu.VMEM), pl.BlockSpec(memory_space=pltpu.HBM)
    n, first = len(pieces), before is None
    arrays, plan = [], []
    for offset, pair, *blocks in pieces:
        numbered = []
        for parts in blocks:
            numbers = []
            for array, index in parts:
                known = [i for i, other in enumerate(arrays) if other is array]
                if not known:
                    arrays.append(array)
                numbers.append(((known or [len(arrays) - 1])[0], index))
            numbered.append(numbers)
        plan.append((offset, pair, numbered))
    sums = jax.ShapeDtypeStruct((LAGS * CH, 256), jnp.float32)
    half = jax.ShapeDtypeStruct((LAGS, 64, 256), jnp.float32)
    scratch = [
        pltpu.VMEM((n, 4, CH, QUARTER + LANES), jnp.bfloat16),
        pltpu.VMEM((n, 256, SPAN), jnp.bfloat16),
        pltpu.SemaphoreType.DMA((n, 8)),
    ]
    return pl.pallas_call(
        make_kernel(plan, len(arrays), first, last),
        out_shape=(half, half) if last else sums,
        in_specs=[pl.BlockSpec(memory_space=pltpu.SMEM)] + [anywhere] * (4 + len(arrays)) + ([] if first else [vmem]),
        out_specs=(vmem, vmem) if last else vmem,
        scratch_shapes=scratch + ([pltpu.VMEM((LAGS * CH, 256), jnp.float32)] if last else []),
        input_output_aliases={} if first or last else {5 + len(arrays): 0},
        compiler_params=pltpu.CompilerParams(vmem_limit_bytes=VLIM * 2**20),
        cost_estimate=pl.CostEstimate(flops=n * 2 * 2048 * 256 * 1024, bytes_accessed=n * 2**20, transcendentals=0),
    )(ix, *rows, *arrays, *([] if first else [before]))


def after(values, done):
    return lax.optimization_barrier((values, done))[0]


def on_device(strain):
    c = lax.axis_index("c")
    own = strain.T
    mine = lax.dynamic_slice(own, (0, c * SPAN), (64, SPAN))
    others = lax.dynamic_slice(own, (0, (1 - c) * SPAN), (64, SPAN))
    got = swap(others, "c", 1, 2)
    block = jnp.where(c == 0, jnp.concatenate([mine, got]), jnp.concatenate([got, mine]))

    quarters = [
        lax.ppermute(block[:, QUARTER * q : QUARTER * (q + 1)], AXES, scatter_pairs(q)) for q in range(4)
    ]
    head = lax.ppermute(block[:, :LANES], ("x", "zl", "c"), [(i, i - 1) for i in range(1, 16)])
    slab = jnp.concatenate([block, head], axis=1)
    slabs = jnp.stack([slab, swap(slab, "zl", 1, 2)])
    held = jnp.concatenate(quarters, axis=1)

    above, below = pull(held, "zh", 1, 4), pull(held, "zh", 3, 4)
    own_1, own_3 = swap(held, "y", 1, 4), swap(held, "y", 3, 4)
    rows_2 = pull(after(slabs, held), "x", 2, 4)

    across = pull(after(held, (own_1, own_3)), "zh", 2, 4)
    above, below, own_1, own_3, slabs = lax.optimization_barrier((above, below, own_1, own_3, slabs))
    via_1 = swap(jnp.stack([above, below]), "y", 1, 4)
    via_3 = swap(jnp.stack([above, below, own_1]), "y", 3, 4)
    rows_1 = pull(slabs, "x", 1, 4)
    rows_3 = pull(after(slabs, rows_2), "x", 3, 4)
    rows = [slabs, rows_1, rows_3, rows_2]

    via_1, via_3, across, *rows = lax.optimization_barrier((via_1, via_3, across, *rows))
    late_1 = swap(jnp.stack([across, via_3[1]]), "y", 1, 4)
    late_3 = swap(jnp.stack([across, via_1[0]]), "y", 3, 4)

    ix = jnp.stack([lax.axis_index(name) for name in AXES]).astype(jnp.int32)
    sums = products(
        ix,
        rows,
        [
            (0, 0, [(held, None)], [(own_1, None)]),
            (0, 1, [(via_3, 2)], [(own_3, None)]),
            (1, 0, [(above, None)], [(via_1, 0)]),
            (3, 0, [(below, None)], [(via_1, 1)]),
        ],
    )
    last_1, last_3 = after((late_1, late_3), sums)
    top, bottom = swap(last_1[0, :64], "y", 3, 4), swap(last_3[0, 64:], "y", 1, 4)
    sums = products(
        ix,
        rows,
        [
            (1, 1, [(late_3, 1)], [(via_3, 0)]),
            (3, 1, [(late_1, 1)], [(via_3, 1)]),
            (2, 0, [(across, None)], [(late_1, 0)]),
        ],
        sums,
    )
    keep, send = products(ix, rows, [(2, 1, [(top, None), (bottom, None)], [(late_3, 0)])], sums, last=True)
    return keep + swap(send, "c", 1, 2)


def solution(mesh):
    fine = Mesh(mesh.devices.reshape(SIZES), AXES)
    return jax.shard_map(
        on_device,
        mesh=fine,
        in_specs=(P(("x", "zl"), ("zh", "y", "c")),),
        out_specs=P(None, ("zh", "y", "c"), ("x", "zl")),
        check_vma=False,
    )
```

```python
import jax
import jax.numpy as jnp
from jax import lax
from jax.experimental import pallas as pl
from jax.experimental.pallas import tpu as pltpu
from jax.sharding import Mesh, PartitionSpec as P

LAGS = 16
TOTAL = 16384
AXES = ("x", "zl", "zh", "y", "c")
SIZES = (4, 2, 4, 4, 2)
CH, SPAN, QUARTER, LANES = 128, 1024, 256, 128
OFFSETS = (0, 1, 3, 2)
ROWS_AT = (0, 1, 3, 2)
VLIM = 14


def device_of(x, zl, zh, y, c):
    return (((x * 2 + zl) * 4 + zh) * 4 + y) * 2 + c


def scatter_pairs(quarter):
    pairs = []
    for x in range(4):
        for zl in range(2):
            for zh in range(4):
                for y in range(4):
                    to_zl = y // 2
                    to_y = y if zl == to_zl else (y + 2) % 4
                    for c in range(2):
                        target = device_of(zh, to_zl, (x + quarter) % 4, to_y, c)
                        pairs.append((device_of(x, zl, zh, y, c), target))
    return pairs


def pull(value, axis, offset, count):
    return lax.ppermute(value, axis, [((i + offset) % count, i) for i in range(count)])


def swap(value, axis, bits, count):
    return lax.ppermute(value, axis, [(i, i ^ bits) for i in range(count)])


def lagged(wide, lags):
    shifted = [jnp.concatenate([window[:, lag : lag + QUARTER] for window in wide], axis=1) for lag in lags]
    return jnp.concatenate(shifted, axis=0)


def make_kernel(pieces, n_arrays, first, share):
    n = len(pieces)

    def kernel(ix, *refs):
        refs = list(refs)
        rows = [refs.pop(0) for _ in OFFSETS]
        arrays = [refs.pop(0) for _ in range(n_arrays)]
        before = None if first else refs.pop(0)
        total, windows, earlier, sems = refs
        x, zl, zh, y, c = (ix[i] for i in range(5))
        half = lax.rem(y, 2)
        away_zl = lax.select(lax.div(y, 2) == zl, 0, 1)
        copies = []
        for i, (offset, pair, blocks) in enumerate(pieces):
            m = away_zl if pair == 0 else 1 - away_zl
            mine = []
            for q in range(4):
                away = lax.rem(zh + offset - q - x + 8, 4)
                for at, slabs in zip(ROWS_AT, rows):
                    source = slabs.at[m, :, pl.ds(QUARTER * q, QUARTER + LANES)]
                    copy = pltpu.make_async_copy(source, windows.at[i, q], sems.at[i, q])
                    pl.when(away == at)(copy.start)
                mine.append(copy)
            for j, (parts, place) in enumerate(zip(blocks, (half, 1 - half))):
                size = CH // len(parts)
                for s, (number, index) in enumerate(parts):
                    start = pl.multiple_of(place * CH + s * size, size)
                    source = arrays[number].at[pl.ds(index, size), :]
                    copy = pltpu.make_async_copy(source, earlier.at[i, pl.ds(start, size), :], sems.at[i, 4 + 2 * j + s])
                    copy.start()
                    mine.append(copy)
            copies.append(mine)
        if share:
            mine = c if share == "keep" else 1 - c
            for copy in copies[0]:
                copy.wait()
            wide = [windows[0, q, pl.ds(pl.multiple_of(mine * 64, 64), 64), :] for q in range(4)]
            for s in range(2):
                part = lax.dot_general(
                    lagged(wide, range(8 * s, 8 * s + 8)), earlier[0], (((1,), (1,)), ((), ())), preferred_element_type=jnp.float32
                )
                for lag in range(8 * s, 8 * s + 8):
                    so_far = before[pl.ds(pl.multiple_of(lag * CH + mine * 64, 64), 64), :]
                    at = (lag - 8 * s) * 64
                    total[lag] = (so_far + part[at : at + 64, :]) * jnp.float32(1.0 / (TOTAL - lag))
            return
        for i in range(n):
            for copy in copies[i]:
                copy.wait()
            wide = [windows[i, q] for q in range(4)]
            for s in range(4):
                span = slice(512 * s, 512 * (s + 1))
                later = lagged(wide, range(4 * s, 4 * s + 4))
                part = lax.dot_general(
                    later, earlier[i], (((1,), (1,)), ((), ())), preferred_element_type=jnp.float32
                )
                if i > 0:
                    total[span, :] += part
                elif first:
                    total[span, :] = part
                else:
                    total[span, :] = before[span, :] + part

    return kernel


def products(ix, rows, pieces, before=None, share=None):
    vmem, anywhere = pl.BlockSpec(memory_space=pltpu.VMEM), pl.BlockSpec(memory_space=pl.ANY)
    n, first = len(pieces), before is None
    arrays, plan = [], []
    for offset, pair, *blocks in pieces:
        numbered = []
        for parts in blocks:
            numbers = []
            for array, index in parts:
                known = [i for i, other in enumerate(arrays) if other is array]
                if not known:
                    arrays.append(array)
                numbers.append(((known or [len(arrays) - 1])[0], index))
            numbered.append(numbers)
        plan.append((offset, pair, numbered))
    sums = jax.ShapeDtypeStruct((LAGS * CH, 256), jnp.float32)
    half = jax.ShapeDtypeStruct((LAGS, 64, 256), jnp.float32)
    scratch = [
        pltpu.VMEM((n, 4, CH, QUARTER + LANES), jnp.bfloat16),
        pltpu.VMEM((n, 256, SPAN), jnp.bfloat16),
        pltpu.SemaphoreType.DMA((n, 8)),
    ]
    return pl.pallas_call(
        make_kernel(plan, len(arrays), first, share),
        out_shape=half if share else sums,
        in_specs=[pl.BlockSpec(memory_space=pltpu.SMEM)] + [anywhere] * (4 + len(arrays)) + ([] if first else [vmem]),
        out_specs=vmem,
        scratch_shapes=scratch,
        input_output_aliases={} if first or share else {5 + len(arrays): 0},
        compiler_params=pltpu.CompilerParams(vmem_limit_bytes=VLIM * 2**20),
        cost_estimate=pl.CostEstimate(flops=n * 2 * 2048 * 256 * 1024, bytes_accessed=n * 2**20, transcendentals=0),
    )(ix, *rows, *arrays, *([] if first else [before]))


def pack(*plans):
    arrays, numbered = [], []
    for plan in plans:
        numbers = []
        for array, first, count in plan:
            known = [i for i, other in enumerate(arrays) if other is array]
            if not known:
                arrays.append(array)
            numbers.append(((known or [len(arrays) - 1])[0], first, count))
        numbered.append(numbers)

    def copy_kernel(*refs):
        sources, targets, sems = refs[: len(arrays)], refs[len(arrays) : -1], refs[-1]
        copies = []
        for target, numbers in zip(targets, numbered):
            at = 0
            for number, first, count in numbers:
                copies.append(
                    pltpu.make_async_copy(
                        sources[number].at[pl.ds(first, count), :], target.at[pl.ds(at, count), :], sems.at[len(copies)]
                    )
                )
                copies[-1].start()
                at += count
        for copy in copies:
            copy.wait()

    anywhere = pl.BlockSpec(memory_space=pl.ANY)
    return pl.pallas_call(
        copy_kernel,
        out_shape=[jax.ShapeDtypeStruct((sum(p[2] for p in plan), SPAN), jnp.bfloat16) for plan in plans],
        in_specs=[anywhere] * len(arrays),
        out_specs=[anywhere] * len(plans),
        scratch_shapes=[pltpu.SemaphoreType.DMA((sum(len(plan) for plan in plans),))],
        compiler_params=pltpu.CompilerParams(vmem_limit_bytes=2**20),
        cost_estimate=pl.CostEstimate(flops=0, bytes_accessed=2**20, transcendentals=0),
    )(*arrays)


def after(values, done):
    return lax.optimization_barrier((values, done))[0]


def on_device(strain):
    c = lax.axis_index("c")
    own = strain.T
    mine = lax.dynamic_slice(own, (0, c * SPAN), (64, SPAN))
    others = lax.dynamic_slice(own, (0, (1 - c) * SPAN), (64, SPAN))
    got = swap(others, "c", 1, 2)
    block = jnp.where(c == 0, jnp.concatenate([mine, got]), jnp.concatenate([got, mine]))

    quarters = [
        lax.ppermute(block[:, QUARTER * q : QUARTER * (q + 1)], AXES, scatter_pairs(q)) for q in range(4)
    ]
    head = lax.ppermute(block[:, :LANES], ("x", "zl", "c"), [(i, i - 1) for i in range(1, 16)])
    slab = jnp.concatenate([block, head], axis=1)
    slabs = jnp.stack([slab, swap(slab, "zl", 1, 2)])
    held = jnp.concatenate(quarters, axis=1)

    above, below = pull(held, "zh", 1, 4), pull(held, "zh", 3, 4)
    held_then, slabs = lax.optimization_barrier((held, slabs))
    own_1, own_3 = swap(held_then, "y", 1, 4), swap(held_then, "y", 3, 4)
    rows_2 = pull(slabs, "x", 2, 4)

    across = pull(after(held, (own_1, own_3)), "zh", 2, 4)
    above, below, own_1, own_3, slabs, rows_2 = lax.optimization_barrier(
        (above, below, own_1, own_3, slabs, rows_2)
    )
    to_1, to_3 = pack([(above, 0, CH), (below, 0, CH)], [(above, 0, CH), (below, 0, CH), (own_1, 0, CH)])
    via_1, via_3 = swap(to_1, "y", 1, 4), swap(to_3, "y", 3, 4)
    rows_1 = pull(slabs, "x", 1, 4)
    rows_3 = pull(slabs, "x", 3, 4)
    rows = [slabs, rows_1, rows_3, rows_2]

    via_1, via_3, across, *rows = lax.optimization_barrier((via_1, via_3, across, *rows))
    to_1, to_3 = pack([(across, 0, CH), (via_3, CH, CH)], [(across, 0, CH), (via_1, 0, CH)])
    late_1, late_3 = swap(to_1, "y", 1, 4), swap(to_3, "y", 3, 4)

    ix = jnp.stack([lax.axis_index(name) for name in AXES]).astype(jnp.int32)
    sums = products(
        ix,
        rows,
        [
            (0, 0, [(held, 0)], [(own_1, 0)]),
            (0, 1, [(via_3, 2 * CH)], [(own_3, 0)]),
            (1, 0, [(above, 0)], [(via_1, 0)]),
            (3, 0, [(below, 0)], [(via_1, CH)]),
        ],
    )
    last_1, last_3 = after((late_1, late_3), sums)
    to_3, to_1 = pack([(last_1, 0, 64)], [(last_3, 64, 64)])
    top, bottom = swap(to_3, "y", 3, 4), swap(to_1, "y", 1, 4)
    sums = products(
        ix,
        rows,
        [
            (1, 1, [(late_3, CH)], [(via_3, 0)]),
            (3, 1, [(late_1, CH)], [(via_3, CH)]),
            (2, 0, [(across, 0)], [(late_1, 0)]),
        ],
        sums,
    )
    final = [(2, 1, [(top, 0), (bottom, 0)], [(late_3, 0)])]
    send = products(ix, rows, final, sums, share="send")
    got = swap(send, "c", 1, 2)
    return products(ix, rows, final, sums, share="keep") + got


def solution(mesh):
    fine = Mesh(mesh.devices.reshape(SIZES), AXES)
    return jax.shard_map(
        on_device,
        mesh=fine,
        in_specs=(P(("x", "zl"), ("zh", "y", "c")),),
        out_specs=P(None, ("zh", "y", "c"), ("x", "zl")),
        check_vma=False,
    )
```

```python
import jax
import jax.numpy as jnp
from jax import lax
from jax.experimental import pallas as pl
from jax.experimental.pallas import tpu as pltpu
from jax.sharding import Mesh, PartitionSpec as P

LAGS = 16
TOTAL = 16384
AXES = ("x", "zl", "zh", "y", "c")
SIZES = (4, 2, 4, 4, 2)
CH, SPAN, QUARTER, LANES = 128, 1024, 256, 128
OFFSETS = (0, 1, 3, 2)
ROWS_AT = (0, 1, 3, 2)
VLIM = 14


def device_of(x, zl, zh, y, c):
    return (((x * 2 + zl) * 4 + zh) * 4 + y) * 2 + c


def scatter_pairs(quarter):
    pairs = []
    for x in range(4):
        for zl in range(2):
            for zh in range(4):
                for y in range(4):
                    to_zl = y // 2
                    to_y = y if zl == to_zl else (y + 2) % 4
                    for c in range(2):
                        target = device_of(zh, to_zl, (x + quarter) % 4, to_y, c)
                        pairs.append((device_of(x, zl, zh, y, c), target))
    return pairs


def pull(value, axis, offset, count):
    return lax.ppermute(value, axis, [((i + offset) % count, i) for i in range(count)])


def swap(value, axis, bits, count):
    return lax.ppermute(value, axis, [(i, i ^ bits) for i in range(count)])


def clear(ref):
    ref[...] = jnp.zeros(ref.shape, ref.dtype)


def heads_of(rows):
    def head_kernel(*refs):
        sources, target, sems = refs[:4], refs[4], refs[5]
        copies = [
            pltpu.make_async_copy(slabs.at[m, :, pl.ds(0, LANES)], target.at[2 * at + m], sems.at[2 * at + m])
            for at, slabs in zip(ROWS_AT, sources)
            for m in range(2)
        ]
        for copy in copies:
            copy.start()
        for copy in copies:
            copy.wait()

    anywhere = pl.BlockSpec(memory_space=pl.ANY)
    return pl.pallas_call(
        head_kernel,
        out_shape=jax.ShapeDtypeStruct((8, CH, LANES), jnp.bfloat16),
        in_specs=[anywhere] * 4,
        out_specs=anywhere,
        scratch_shapes=[pltpu.SemaphoreType.DMA((8,))],
        compiler_params=pltpu.CompilerParams(vmem_limit_bytes=2**20),
        cost_estimate=pl.CostEstimate(flops=0, bytes_accessed=2**19, transcendentals=0),
    )(*rows)


def lagged(wide, lags):
    shifted = [jnp.concatenate([window[:, lag : lag + QUARTER] for window in wide], axis=1) for lag in lags]
    return jnp.concatenate(shifted, axis=0)


def make_kernel(pieces, n_arrays, first, share):
    n = len(pieces)

    def kernel(ix, *refs):
        refs = list(refs)
        rows, heads = [refs.pop(0) for _ in OFFSETS], refs.pop(0)
        arrays = [refs.pop(0) for _ in range(n_arrays)]
        before = None if first else refs.pop(0)
        total, windows, earlier, sems = refs
        x, zl, zh, y, c = (ix[i] for i in range(5))
        half = lax.rem(y, 2)
        away_zl = lax.select(lax.div(y, 2) == zl, 0, 1)
        copies, ends = [], []
        for i, (offset, pair, blocks) in enumerate(pieces):
            m = away_zl if pair == 0 else 1 - away_zl
            mine = []
            for q in range(4):
                away = lax.rem(zh + offset - q - x + 8, 4)
                width = QUARTER + LANES if q < 3 else QUARTER
                for at, slabs in zip(ROWS_AT, rows):
                    source = slabs.at[m, :, pl.ds(QUARTER * q, width)]
                    copy = pltpu.make_async_copy(source, windows.at[i, q, :, pl.ds(0, width)], sems.at[i, q])
                    pl.when(away == at)(copy.start)
                mine.append(copy)
            zl_slab = lax.rem(zl + m, 2)
            onward = c * zl_slab
            head = 2 * lax.rem(away + onward, 4) + lax.select(c == 0, m, 1 - m)
            copy = pltpu.make_async_copy(heads.at[head], windows.at[i, 3, :, pl.ds(QUARTER, LANES)], sems.at[i, 8])
            copy.start()
            mine.append(copy)
            ends.append((onward == 1) & (lax.rem(zh + offset - 3 + 8, 4) == 3))
            for j, (parts, place) in enumerate(zip(blocks, (half, 1 - half))):
                size = CH // len(parts)
                for s, (number, index) in enumerate(parts):
                    start = pl.multiple_of(place * CH + s * size, size)
                    source = arrays[number].at[pl.ds(index, size), :]
                    copy = pltpu.make_async_copy(source, earlier.at[i, pl.ds(start, size), :], sems.at[i, 4 + 2 * j + s])
                    copy.start()
                    mine.append(copy)
            copies.append(mine)
        if share:
            mine = c if share == "keep" else 1 - c
            for copy in copies[0]:
                copy.wait()
            pl.when(ends[0])(lambda: clear(windows.at[0, 3, :, pl.ds(QUARTER, LANES)]))
            wide = [windows[0, q, pl.ds(pl.multiple_of(mine * 64, 64), 64), :] for q in range(4)]
            for s in range(2):
                part = lax.dot_general(
                    lagged(wide, range(8 * s, 8 * s + 8)), earlier[0], (((1,), (1,)), ((), ())), preferred_element_type=jnp.float32
                )
                for lag in range(8 * s, 8 * s + 8):
                    so_far = before[pl.ds(pl.multiple_of(lag * CH + mine * 64, 64), 64), :]
                    at = (lag - 8 * s) * 64
                    total[lag] = (so_far + part[at : at + 64, :]) * jnp.float32(1.0 / (TOTAL - lag))
            return
        for i in range(n):
            for copy in copies[i]:
                copy.wait()
            pl.when(ends[i])(lambda i=i: clear(windows.at[i, 3, :, pl.ds(QUARTER, LANES)]))
            wide = [windows[i, q] for q in range(4)]
            for s in range(4):
                span = slice(512 * s, 512 * (s + 1))
                later = lagged(wide, range(4 * s, 4 * s + 4))
                part = lax.dot_general(
                    later, earlier[i], (((1,), (1,)), ((), ())), preferred_element_type=jnp.float32
                )
                if i > 0:
                    total[span, :] += part
                elif first:
                    total[span, :] = part
                else:
                    total[span, :] = before[span, :] + part

    return kernel


def products(ix, rows, pieces, before=None, share=None):
    vmem, anywhere = pl.BlockSpec(memory_space=pltpu.VMEM), pl.BlockSpec(memory_space=pl.ANY)
    n, first = len(pieces), before is None
    arrays, plan = [], []
    for offset, pair, *blocks in pieces:
        numbered = []
        for parts in blocks:
            numbers = []
            for array, index in parts:
                known = [i for i, other in enumerate(arrays) if other is array]
                if not known:
                    arrays.append(array)
                numbers.append(((known or [len(arrays) - 1])[0], index))
            numbered.append(numbers)
        plan.append((offset, pair, numbered))
    sums = jax.ShapeDtypeStruct((LAGS * CH, 256), jnp.float32)
    half = jax.ShapeDtypeStruct((LAGS, 64, 256), jnp.float32)
    scratch = [
        pltpu.VMEM((n, 4, CH, QUARTER + LANES), jnp.bfloat16),
        pltpu.VMEM((n, 256, SPAN), jnp.bfloat16),
        pltpu.SemaphoreType.DMA((n, 9)),
    ]
    return pl.pallas_call(
        make_kernel(plan, len(arrays), first, share),
        out_shape=half if share else sums,
        in_specs=[pl.BlockSpec(memory_space=pltpu.SMEM)] + [anywhere] * (5 + len(arrays)) + ([] if first else [vmem]),
        out_specs=vmem,
        scratch_shapes=scratch,
        input_output_aliases={} if first or share else {6 + len(arrays): 0},
        compiler_params=pltpu.CompilerParams(vmem_limit_bytes=VLIM * 2**20),
        cost_estimate=pl.CostEstimate(flops=n * 2 * 2048 * 256 * 1024, bytes_accessed=n * 2**20, transcendentals=0),
    )(ix, *rows, *arrays, *([] if first else [before]))


def pack(*plans):
    arrays, numbered = [], []
    for plan in plans:
        numbers = []
        for array, first, count in plan:
            known = [i for i, other in enumerate(arrays) if other is array]
            if not known:
                arrays.append(array)
            numbers.append(((known or [len(arrays) - 1])[0], first, count))
        numbered.append(numbers)

    def copy_kernel(*refs):
        sources, targets, sems = refs[: len(arrays)], refs[len(arrays) : -1], refs[-1]
        copies = []
        for target, numbers in zip(targets, numbered):
            at = 0
            for number, first, count in numbers:
                copies.append(
                    pltpu.make_async_copy(
                        sources[number].at[pl.ds(first, count), :], target.at[pl.ds(at, count), :], sems.at[len(copies)]
                    )
                )
                copies[-1].start()
                at += count
        for copy in copies:
            copy.wait()

    anywhere = pl.BlockSpec(memory_space=pl.ANY)
    return pl.pallas_call(
        copy_kernel,
        out_shape=[jax.ShapeDtypeStruct((sum(p[2] for p in plan), SPAN), jnp.bfloat16) for plan in plans],
        in_specs=[anywhere] * len(arrays),
        out_specs=[anywhere] * len(plans),
        scratch_shapes=[pltpu.SemaphoreType.DMA((sum(len(plan) for plan in plans),))],
        compiler_params=pltpu.CompilerParams(vmem_limit_bytes=2**20),
        cost_estimate=pl.CostEstimate(flops=0, bytes_accessed=2**20, transcendentals=0),
    )(*arrays)


def after(values, done):
    return lax.optimization_barrier((values, done))[0]


def on_device(strain):
    c = lax.axis_index("c")
    own = strain.T
    mine = lax.dynamic_slice(own, (0, c * SPAN), (64, SPAN))
    others = lax.dynamic_slice(own, (0, (1 - c) * SPAN), (64, SPAN))
    got = swap(others, "c", 1, 2)
    block = jnp.where(c == 0, jnp.concatenate([mine, got]), jnp.concatenate([got, mine]))

    quarters = [
        lax.ppermute(block[:, QUARTER * q : QUARTER * (q + 1)], AXES, scatter_pairs(q)) for q in range(4)
    ]
    slabs = jnp.stack([block, swap(block, "zl", 1, 2)])
    held = jnp.concatenate(quarters, axis=1)

    above, below = pull(held, "zh", 1, 4), pull(held, "zh", 3, 4)
    held_then, slabs = lax.optimization_barrier((held, slabs))
    own_1, own_3 = swap(held_then, "y", 1, 4), swap(held_then, "y", 3, 4)
    rows_2 = pull(slabs, "x", 2, 4)

    across = pull(after(held, (own_1, own_3)), "zh", 2, 4)
    above, below, own_1, own_3, slabs, rows_2 = lax.optimization_barrier(
        (above, below, own_1, own_3, slabs, rows_2)
    )
    to_1, to_3 = pack([(above, 0, CH), (below, 0, CH)], [(above, 0, CH), (below, 0, CH), (own_1, 0, CH)])
    via_1, via_3 = swap(to_1, "y", 1, 4), swap(to_3, "y", 3, 4)
    rows_1 = pull(slabs, "x", 1, 4)
    rows_3 = pull(slabs, "x", 3, 4)
    rows = [slabs, rows_1, rows_3, rows_2]

    via_1, via_3, across, *rows = lax.optimization_barrier((via_1, via_3, across, *rows))
    rows = [*rows, swap(heads_of(rows), "c", 1, 2)]
    to_1, to_3 = pack([(across, 0, CH), (via_3, CH, CH)], [(across, 0, CH), (via_1, 0, CH)])
    late_1, late_3 = swap(to_1, "y", 1, 4), swap(to_3, "y", 3, 4)

    ix = jnp.stack([lax.axis_index(name) for name in AXES]).astype(jnp.int32)
    sums = products(
        ix,
        rows,
        [
            (0, 0, [(held, 0)], [(own_1, 0)]),
            (0, 1, [(via_3, 2 * CH)], [(own_3, 0)]),
            (1, 0, [(above, 0)], [(via_1, 0)]),
            (3, 0, [(below, 0)], [(via_1, CH)]),
        ],
    )
    last_1, last_3 = after((late_1, late_3), sums)
    to_3, to_1 = pack([(last_1, 0, 64)], [(last_3, 64, 64)])
    top, bottom = swap(to_3, "y", 3, 4), swap(to_1, "y", 1, 4)
    sums = products(
        ix,
        rows,
        [
            (1, 1, [(late_3, CH)], [(via_3, 0)]),
            (3, 1, [(late_1, CH)], [(via_3, CH)]),
            (2, 0, [(across, 0)], [(late_1, 0)]),
        ],
        sums,
    )
    final = [(2, 1, [(top, 0), (bottom, 0)], [(late_3, 0)])]
    send = products(ix, rows, final, sums, share="send")
    got = swap(send, "c", 1, 2)
    return products(ix, rows, final, sums, share="keep") + got


def solution(mesh):
    fine = Mesh(mesh.devices.reshape(SIZES), AXES)
    return jax.shard_map(
        on_device,
        mesh=fine,
        in_specs=(P(("x", "zl"), ("zh", "y", "c")),),
        out_specs=P(None, ("zh", "y", "c"), ("x", "zl")),
        check_vma=False,
    )
```

```python
import jax
import jax.numpy as jnp
from jax import lax
from jax.experimental import pallas as pl
from jax.experimental.pallas import tpu as pltpu
from jax.sharding import Mesh, PartitionSpec as P

LAGS = 16
TOTAL = 16384
AXES = ("x", "zl", "zh", "y", "c")
SIZES = (4, 2, 4, 4, 2)
CH, SPAN, QUARTER, LANES = 128, 1024, 256, 128
OFFSETS = (0, 1, 3, 2)
ROWS_AT = (0, 1, 3, 2)
VLIM = 14


def device_of(x, zl, zh, y, c):
    return (((x * 2 + zl) * 4 + zh) * 4 + y) * 2 + c


def scatter_pairs(quarter):
    pairs = []
    for x in range(4):
        for zl in range(2):
            for zh in range(4):
                for y in range(4):
                    to_zl = y // 2
                    to_y = y if zl == to_zl else (y + 2) % 4
                    for c in range(2):
                        target = device_of(zh, to_zl, (x + quarter) % 4, to_y, c)
                        pairs.append((device_of(x, zl, zh, y, c), target))
    return pairs


def pull(value, axis, offset, count):
    return lax.ppermute(value, axis, [((i + offset) % count, i) for i in range(count)])


def swap(value, axis, bits, count):
    return lax.ppermute(value, axis, [(i, i ^ bits) for i in range(count)])


def clear(ref):
    ref[...] = jnp.zeros(ref.shape, ref.dtype)


def heads_of(rows):
    def head_kernel(*refs):
        sources, target, sems = refs[:4], refs[4], refs[5]
        copies = [
            pltpu.make_async_copy(slabs.at[m, :, pl.ds(0, LANES)], target.at[2 * at + m], sems.at[2 * at + m])
            for at, slabs in zip(ROWS_AT, sources)
            for m in range(2)
        ]
        for copy in copies:
            copy.start()
        for copy in copies:
            copy.wait()

    anywhere = pl.BlockSpec(memory_space=pl.ANY)
    return pl.pallas_call(
        head_kernel,
        out_shape=jax.ShapeDtypeStruct((8, CH, LANES), jnp.bfloat16),
        in_specs=[anywhere] * 4,
        out_specs=anywhere,
        scratch_shapes=[pltpu.SemaphoreType.DMA((8,))],
        compiler_params=pltpu.CompilerParams(vmem_limit_bytes=2**20),
        cost_estimate=pl.CostEstimate(flops=0, bytes_accessed=2**19, transcendentals=0),
    )(*rows)


def lagged(wide, lags):
    shifted = [jnp.concatenate([window[:, lag : lag + QUARTER] for window in wide], axis=1) for lag in lags]
    return jnp.concatenate(shifted, axis=0)


def make_kernel(pieces, n_arrays, first, share):
    n = len(pieces)

    def kernel(ix, *refs):
        refs = list(refs)
        rows, heads = [refs.pop(0) for _ in OFFSETS], refs.pop(0)
        arrays = [refs.pop(0) for _ in range(n_arrays)]
        before = None if first else refs.pop(0)
        total, windows, earlier, sems = refs
        x, zl, zh, y, c = (ix[i] for i in range(5))
        half = lax.rem(y, 2)
        away_zl = lax.select(lax.div(y, 2) == zl, 0, 1)
        copies, ends = [], []
        for i, (offset, pair, blocks) in enumerate(pieces):
            m = away_zl if pair == 0 else 1 - away_zl
            mine = []
            for q in range(4):
                away = lax.rem(zh + offset - q - x + 8, 4)
                width = QUARTER + LANES if q < 3 else QUARTER
                for at, slabs in zip(ROWS_AT, rows):
                    source = slabs.at[m, :, pl.ds(QUARTER * q, width)]
                    copy = pltpu.make_async_copy(source, windows.at[i, q, :, pl.ds(0, width)], sems.at[i, q])
                    pl.when(away == at)(copy.start)
                mine.append(copy)
            zl_slab = lax.rem(zl + m, 2)
            onward = c * zl_slab
            head = 2 * lax.rem(away + onward, 4) + lax.select(c == 0, m, 1 - m)
            copy = pltpu.make_async_copy(heads.at[head], windows.at[i, 3, :, pl.ds(QUARTER, LANES)], sems.at[i, 8])
            copy.start()
            mine.append(copy)
            ends.append((onward == 1) & (lax.rem(zh + offset - 3 + 8, 4) == 3))
            for j, (parts, place) in enumerate(zip(blocks, (half, 1 - half))):
                size = CH // len(parts)
                for s, (number, index) in enumerate(parts):
                    start = pl.multiple_of(place * CH + s * size, size)
                    source = arrays[number].at[pl.ds(index, size), :]
                    copy = pltpu.make_async_copy(source, earlier.at[i, pl.ds(start, size), :], sems.at[i, 4 + 2 * j + s])
                    copy.start()
                    mine.append(copy)
            copies.append(mine)
        if share:
            mine = c if share == "keep" else 1 - c
            for copy in copies[0]:
                copy.wait()
            pl.when(ends[0])(lambda: clear(windows.at[0, 3, :, pl.ds(QUARTER, LANES)]))
            wide = [windows[0, q, pl.ds(pl.multiple_of(mine * 64, 64), 64), :] for q in range(4)]
            for s in range(2):
                part = lax.dot_general(
                    lagged(wide, range(8 * s, 8 * s + 8)), earlier[0], (((1,), (1,)), ((), ())), preferred_element_type=jnp.float32
                )
                for lag in range(8 * s, 8 * s + 8):
                    so_far = before[pl.ds(pl.multiple_of(lag * CH + mine * 64, 64), 64), :]
                    at = (lag - 8 * s) * 64
                    total[lag] = (so_far + part[at : at + 64, :]) * jnp.float32(1.0 / (TOTAL - lag))
            return
        for i in range(n):
            for copy in copies[i]:
                copy.wait()
            pl.when(ends[i])(lambda i=i: clear(windows.at[i, 3, :, pl.ds(QUARTER, LANES)]))
            wide = [windows[i, q] for q in range(4)]
            for s in range(4):
                span = slice(512 * s, 512 * (s + 1))
                later = lagged(wide, range(4 * s, 4 * s + 4))
                part = lax.dot_general(
                    later, earlier[i], (((1,), (1,)), ((), ())), preferred_element_type=jnp.float32
                )
                if i > 0:
                    total[span, :] += part
                elif first:
                    total[span, :] = part
                else:
                    total[span, :] = before[span, :] + part

    return kernel


def products(ix, rows, pieces, before=None, share=None):
    vmem, anywhere = pl.BlockSpec(memory_space=pltpu.VMEM), pl.BlockSpec(memory_space=pl.ANY)
    n, first = len(pieces), before is None
    arrays, plan = [], []
    for offset, pair, *blocks in pieces:
        numbered = []
        for parts in blocks:
            numbers = []
            for array, index in parts:
                known = [i for i, other in enumerate(arrays) if other is array]
                if not known:
                    arrays.append(array)
                numbers.append(((known or [len(arrays) - 1])[0], index))
            numbered.append(numbers)
        plan.append((offset, pair, numbered))
    sums = jax.ShapeDtypeStruct((LAGS * CH, 256), jnp.float32)
    half = jax.ShapeDtypeStruct((LAGS, 64, 256), jnp.float32)
    scratch = [
        pltpu.VMEM((n, 4, CH, QUARTER + LANES), jnp.bfloat16),
        pltpu.VMEM((n, 256, SPAN), jnp.bfloat16),
        pltpu.SemaphoreType.DMA((n, 9)),
    ]
    return pl.pallas_call(
        make_kernel(plan, len(arrays), first, share),
        out_shape=half if share else sums,
        in_specs=[pl.BlockSpec(memory_space=pltpu.SMEM)] + [anywhere] * (5 + len(arrays)) + ([] if first else [vmem]),
        out_specs=vmem,
        scratch_shapes=scratch,
        input_output_aliases={} if first or share else {6 + len(arrays): 0},
        compiler_params=pltpu.CompilerParams(vmem_limit_bytes=VLIM * 2**20),
        cost_estimate=pl.CostEstimate(flops=n * 2 * 2048 * 256 * 1024, bytes_accessed=n * 2**20, transcendentals=0),
    )(ix, *rows, *arrays, *([] if first else [before]))


def pack(*plans):
    arrays, numbered = [], []
    for plan in plans:
        numbers = []
        for array, first, count in plan:
            known = [i for i, other in enumerate(arrays) if other is array]
            if not known:
                arrays.append(array)
            numbers.append(((known or [len(arrays) - 1])[0], first, count))
        numbered.append(numbers)

    def copy_kernel(*refs):
        sources, targets, sems = refs[: len(arrays)], refs[len(arrays) : -1], refs[-1]
        copies = []
        for target, numbers in zip(targets, numbered):
            at = 0
            for number, first, count in numbers:
                copies.append(
                    pltpu.make_async_copy(
                        sources[number].at[pl.ds(first, count), :], target.at[pl.ds(at, count), :], sems.at[len(copies)]
                    )
                )
                copies[-1].start()
                at += count
        for copy in copies:
            copy.wait()

    anywhere = pl.BlockSpec(memory_space=pl.ANY)
    return pl.pallas_call(
        copy_kernel,
        out_shape=[jax.ShapeDtypeStruct((sum(p[2] for p in plan), SPAN), jnp.bfloat16) for plan in plans],
        in_specs=[anywhere] * len(arrays),
        out_specs=[anywhere] * len(plans),
        scratch_shapes=[pltpu.SemaphoreType.DMA((sum(len(plan) for plan in plans),))],
        compiler_params=pltpu.CompilerParams(vmem_limit_bytes=2**20),
        cost_estimate=pl.CostEstimate(flops=0, bytes_accessed=2**20, transcendentals=0),
    )(*arrays)


def after(values, done):
    return lax.optimization_barrier((values, done))[0]


def on_device(strain):
    c = lax.axis_index("c")
    own = strain.T
    mine = lax.dynamic_slice(own, (0, c * SPAN), (64, SPAN))
    others = lax.dynamic_slice(own, (0, (1 - c) * SPAN), (64, SPAN))
    got = swap(others, "c", 1, 2)
    block = jnp.where(c == 0, jnp.concatenate([mine, got]), jnp.concatenate([got, mine]))

    quarters = [
        lax.ppermute(block[:, QUARTER * q : QUARTER * (q + 1)], AXES, scatter_pairs(q)) for q in range(4)
    ]
    slabs = jnp.stack([block, swap(block, "zl", 1, 2)])
    held = jnp.concatenate(quarters, axis=1)

    above, below = pull(held, "zh", 1, 4), pull(held, "zh", 3, 4)
    own_1, own_3 = swap(held, "y", 1, 4), swap(held, "y", 3, 4)
    rows_2 = pull(slabs, "x", 2, 4)

    across = pull(after(held, (own_1, own_3)), "zh", 2, 4)
    above, below, own_1, own_3, slabs, rows_2 = lax.optimization_barrier(
        (above, below, own_1, own_3, slabs, rows_2)
    )
    to_1, to_3 = pack([(above, 0, CH), (below, 0, CH)], [(above, 0, CH), (below, 0, CH), (own_1, 0, CH)])
    via_1, via_3 = swap(to_1, "y", 1, 4), swap(to_3, "y", 3, 4)
    rows_1 = pull(slabs, "x", 1, 4)
    rows_3 = pull(slabs, "x", 3, 4)
    rows = [slabs, rows_1, rows_3, rows_2]

    via_1, via_3, across, *rows = lax.optimization_barrier((via_1, via_3, across, *rows))
    rows = [*rows, swap(heads_of(rows), "c", 1, 2)]
    to_1, to_3 = pack([(across, 0, CH), (via_3, CH, CH)], [(across, 0, CH), (via_1, 0, CH)])
    late_1, late_3 = swap(to_1, "y", 1, 4), swap(to_3, "y", 3, 4)

    ix = jnp.stack([lax.axis_index(name) for name in AXES]).astype(jnp.int32)
    sums = products(
        ix,
        rows,
        [
            (0, 0, [(held, 0)], [(own_1, 0)]),
            (0, 1, [(via_3, 2 * CH)], [(own_3, 0)]),
            (1, 0, [(above, 0)], [(via_1, 0)]),
            (3, 0, [(below, 0)], [(via_1, CH)]),
        ],
    )
    last_1, last_3 = after((late_1, late_3), sums)
    to_3, to_1 = pack([(last_1, 0, 64)], [(last_3, 64, 64)])
    top, bottom = swap(to_3, "y", 3, 4), swap(to_1, "y", 1, 4)
    sums = products(
        ix,
        rows,
        [
            (1, 1, [(late_3, CH)], [(via_3, 0)]),
            (3, 1, [(late_1, CH)], [(via_3, CH)]),
            (2, 0, [(across, 0)], [(late_1, 0)]),
        ],
        sums,
    )
    final = [(2, 1, [(top, 0), (bottom, 0)], [(late_3, 0)])]
    send = products(ix, rows, final, sums, share="send")
    got = swap(send, "c", 1, 2)
    return products(ix, rows, final, sums, share="keep") + got


def solution(mesh):
    fine = Mesh(mesh.devices.reshape(SIZES), AXES)
    return jax.shard_map(
        on_device,
        mesh=fine,
        in_specs=(P(("x", "zl"), ("zh", "y", "c")),),
        out_specs=P(None, ("zh", "y", "c"), ("x", "zl")),
        check_vma=False,
    )
```

```python
import jax
import jax.numpy as jnp
from jax import lax
from jax.experimental import pallas as pl
from jax.experimental.pallas import tpu as pltpu
from jax.sharding import Mesh, PartitionSpec as P

LAGS = 16
TOTAL = 16384
AXES = ("x", "zl", "zh", "y", "c")
SIZES = (4, 2, 4, 4, 2)
CH, SPAN, QUARTER, LANES = 128, 1024, 256, 128
OFFSETS = (0, 1, 3, 2)
ROWS_AT = (0, 1, 3, 2)
VLIM = 14


def device_of(x, zl, zh, y, c):
    return (((x * 2 + zl) * 4 + zh) * 4 + y) * 2 + c


def scatter_pairs(quarter):
    pairs = []
    for x in range(4):
        for zl in range(2):
            for zh in range(4):
                for y in range(4):
                    to_zl = y // 2
                    to_y = y if zl == to_zl else (y + 2) % 4
                    for c in range(2):
                        target = device_of(zh, to_zl, (x + quarter) % 4, to_y, c)
                        pairs.append((device_of(x, zl, zh, y, c), target))
    return pairs


def pull(value, axis, offset, count):
    return lax.ppermute(value, axis, [((i + offset) % count, i) for i in range(count)])


def swap(value, axis, bits, count):
    return lax.ppermute(value, axis, [(i, i ^ bits) for i in range(count)])


def clear(ref):
    ref[...] = jnp.zeros(ref.shape, ref.dtype)


def heads_of(rows):
    def head_kernel(*refs):
        sources, target, sems = refs[:4], refs[4], refs[5]
        copies = [
            pltpu.make_async_copy(slabs.at[m, :, pl.ds(0, LANES)], target.at[2 * at + m], sems.at[2 * at + m])
            for at, slabs in zip(ROWS_AT, sources)
            for m in range(2)
        ]
        for copy in copies:
            copy.start()
        for copy in copies:
            copy.wait()

    anywhere = pl.BlockSpec(memory_space=pl.ANY)
    return pl.pallas_call(
        head_kernel,
        out_shape=jax.ShapeDtypeStruct((8, CH, LANES), jnp.bfloat16),
        in_specs=[anywhere] * 4,
        out_specs=anywhere,
        scratch_shapes=[pltpu.SemaphoreType.DMA((8,))],
        compiler_params=pltpu.CompilerParams(vmem_limit_bytes=2**20),
        cost_estimate=pl.CostEstimate(flops=0, bytes_accessed=2**19, transcendentals=0),
    )(*rows)


def lagged(wide, lags):
    shifted = [jnp.concatenate([window[:, lag : lag + QUARTER] for window in wide], axis=1) for lag in lags]
    return jnp.concatenate(shifted, axis=0)


def make_kernel(pieces, n_arrays, first, share):
    n = len(pieces)

    def kernel(ix, *refs):
        refs = list(refs)
        rows, heads = [refs.pop(0) for _ in OFFSETS], refs.pop(0)
        arrays = [refs.pop(0) for _ in range(n_arrays)]
        before = None if first else refs.pop(0)
        total, windows, earlier, sems = refs
        x, zl, zh, y, c = (ix[i] for i in range(5))
        half = lax.rem(y, 2)
        away_zl = lax.select(lax.div(y, 2) == zl, 0, 1)
        copies, ends = [], []
        for i, (offset, pair, blocks) in enumerate(pieces):
            m = away_zl if pair == 0 else 1 - away_zl
            mine = []
            for q in range(4):
                away = lax.rem(zh + offset - q - x + 8, 4)
                width = QUARTER + LANES if q < 3 else QUARTER
                for at, slabs in zip(ROWS_AT, rows):
                    source = slabs.at[m, :, pl.ds(QUARTER * q, width)]
                    copy = pltpu.make_async_copy(source, windows.at[i, q, :, pl.ds(0, width)], sems.at[i, q])
                    pl.when(away == at)(copy.start)
                mine.append(copy)
            zl_slab = lax.rem(zl + m, 2)
            onward = c * zl_slab
            head = 2 * lax.rem(away + onward, 4) + lax.select(c == 0, m, 1 - m)
            copy = pltpu.make_async_copy(heads.at[head], windows.at[i, 3, :, pl.ds(QUARTER, LANES)], sems.at[i, 8])
            copy.start()
            mine.append(copy)
            ends.append((onward == 1) & (lax.rem(zh + offset - 3 + 8, 4) == 3))
            for j, (parts, place) in enumerate(zip(blocks, (half, 1 - half))):
                size = CH // len(parts)
                for s, (number, index) in enumerate(parts):
                    start = pl.multiple_of(place * CH + s * size, size)
                    source = arrays[number].at[pl.ds(index, size), :]
                    copy = pltpu.make_async_copy(source, earlier.at[i, pl.ds(start, size), :], sems.at[i, 4 + 2 * j + s])
                    copy.start()
                    mine.append(copy)
            copies.append(mine)
        if share:
            mine = c if share == "keep" else 1 - c
            for copy in copies[0]:
                copy.wait()
            pl.when(ends[0])(lambda: clear(windows.at[0, 3, :, pl.ds(QUARTER, LANES)]))
            wide = [windows[0, q, pl.ds(pl.multiple_of(mine * 64, 64), 64), :] for q in range(4)]
            for s in range(2):
                part = lax.dot_general(
                    lagged(wide, range(8 * s, 8 * s + 8)), earlier[0], (((1,), (1,)), ((), ())), preferred_element_type=jnp.float32
                )
                for lag in range(8 * s, 8 * s + 8):
                    so_far = before[pl.ds(pl.multiple_of(lag * CH + mine * 64, 64), 64), :]
                    at = (lag - 8 * s) * 64
                    total[lag] = (so_far + part[at : at + 64, :]) * jnp.float32(1.0 / (TOTAL - lag))
            return
        for i in range(n):
            for copy in copies[i]:
                copy.wait()
            pl.when(ends[i])(lambda i=i: clear(windows.at[i, 3, :, pl.ds(QUARTER, LANES)]))
            wide = [windows[i, q] for q in range(4)]
            for s in range(4):
                span = slice(512 * s, 512 * (s + 1))
                later = lagged(wide, range(4 * s, 4 * s + 4))
                part = lax.dot_general(
                    later, earlier[i], (((1,), (1,)), ((), ())), preferred_element_type=jnp.float32
                )
                if i > 0:
                    total[span, :] += part
                elif first:
                    total[span, :] = part
                else:
                    total[span, :] = before[span, :] + part

    return kernel


def products(ix, rows, pieces, before=None, share=None):
    vmem, anywhere = pl.BlockSpec(memory_space=pltpu.VMEM), pl.BlockSpec(memory_space=pl.ANY)
    n, first = len(pieces), before is None
    arrays, plan = [], []
    for offset, pair, *blocks in pieces:
        numbered = []
        for parts in blocks:
            numbers = []
            for array, index in parts:
                known = [i for i, other in enumerate(arrays) if other is array]
                if not known:
                    arrays.append(array)
                numbers.append(((known or [len(arrays) - 1])[0], index))
            numbered.append(numbers)
        plan.append((offset, pair, numbered))
    sums = jax.ShapeDtypeStruct((LAGS * CH, 256), jnp.float32)
    half = jax.ShapeDtypeStruct((LAGS, 64, 256), jnp.float32)
    scratch = [
        pltpu.VMEM((n, 4, CH, QUARTER + LANES), jnp.bfloat16),
        pltpu.VMEM((n, 256, SPAN), jnp.bfloat16),
        pltpu.SemaphoreType.DMA((n, 9)),
    ]
    return pl.pallas_call(
        make_kernel(plan, len(arrays), first, share),
        out_shape=half if share else sums,
        in_specs=[pl.BlockSpec(memory_space=pltpu.SMEM)] + [anywhere] * (5 + len(arrays)) + ([] if first else [vmem]),
        out_specs=vmem,
        scratch_shapes=scratch,
        input_output_aliases={} if first or share else {6 + len(arrays): 0},
        compiler_params=pltpu.CompilerParams(vmem_limit_bytes=VLIM * 2**20),
        cost_estimate=pl.CostEstimate(flops=n * 2 * 2048 * 256 * 1024, bytes_accessed=n * 2**20, transcendentals=0),
    )(ix, *rows, *arrays, *([] if first else [before]))


def pack(*plans):
    arrays, numbered = [], []
    for plan in plans:
        numbers = []
        for array, first, count in plan:
            known = [i for i, other in enumerate(arrays) if other is array]
            if not known:
                arrays.append(array)
            numbers.append(((known or [len(arrays) - 1])[0], first, count))
        numbered.append(numbers)

    def copy_kernel(*refs):
        sources, targets, sems = refs[: len(arrays)], refs[len(arrays) : -1], refs[-1]
        copies = []
        for target, numbers in zip(targets, numbered):
            at = 0
            for number, first, count in numbers:
                copies.append(
                    pltpu.make_async_copy(
                        sources[number].at[pl.ds(first, count), :], target.at[pl.ds(at, count), :], sems.at[len(copies)]
                    )
                )
                copies[-1].start()
                at += count
        for copy in copies:
            copy.wait()

    anywhere = pl.BlockSpec(memory_space=pl.ANY)
    return pl.pallas_call(
        copy_kernel,
        out_shape=[jax.ShapeDtypeStruct((sum(p[2] for p in plan), SPAN), jnp.bfloat16) for plan in plans],
        in_specs=[anywhere] * len(arrays),
        out_specs=[anywhere] * len(plans),
        scratch_shapes=[pltpu.SemaphoreType.DMA((sum(len(plan) for plan in plans),))],
        compiler_params=pltpu.CompilerParams(vmem_limit_bytes=2**20),
        cost_estimate=pl.CostEstimate(flops=0, bytes_accessed=2**20, transcendentals=0),
    )(*arrays)


def after(values, done):
    return lax.optimization_barrier((values, done))[0]


def on_device(strain):
    c = lax.axis_index("c")
    own = strain.T
    mine = lax.dynamic_slice(own, (0, c * SPAN), (64, SPAN))
    others = lax.dynamic_slice(own, (0, (1 - c) * SPAN), (64, SPAN))
    got = swap(others, "c", 1, 2)
    block = jnp.where(c == 0, jnp.concatenate([mine, got]), jnp.concatenate([got, mine]))

    quarters = [
        lax.ppermute(block[:, QUARTER * q : QUARTER * (q + 1)], AXES, scatter_pairs(q)) for q in range(4)
    ]
    slabs = jnp.stack([block, swap(block, "zl", 1, 2)])
    held = jnp.concatenate(quarters, axis=1)

    above, below = pull(held, "zh", 1, 4), pull(held, "zh", 3, 4)
    own_1, own_3 = swap(held, "y", 1, 4), swap(held, "y", 3, 4)
    rows_2 = pull(slabs, "x", 2, 4)

    across = pull(after(held, (own_1, own_3)), "zh", 2, 4)
    above, below, own_1, own_3, slabs, rows_2 = lax.optimization_barrier(
        (above, below, own_1, own_3, slabs, rows_2)
    )
    to_1, to_3 = pack([(above, 0, CH), (below, 0, CH)], [(above, 0, CH), (below, 0, CH), (own_1, 0, CH)])
    via_1, via_3 = swap(to_1, "y", 1, 4), swap(to_3, "y", 3, 4)
    rows_1 = pull(slabs, "x", 1, 4)
    rows_3 = pull(slabs, "x", 3, 4)
    rows = [slabs, rows_1, rows_3, rows_2]

    rows = [*rows, swap(heads_of(rows), "c", 1, 2)]
    to_1, to_3 = pack([(across, 0, CH), (via_3, CH, CH)], [(across, 0, CH), (via_1, 0, CH)])
    late_1, late_3 = swap(to_1, "y", 1, 4), swap(to_3, "y", 3, 4)

    ix = jnp.stack([lax.axis_index(name) for name in AXES]).astype(jnp.int32)
    sums = products(
        ix,
        rows,
        [
            (0, 0, [(held, 0)], [(own_1, 0)]),
            (0, 1, [(via_3, 2 * CH)], [(own_3, 0)]),
            (1, 0, [(above, 0)], [(via_1, 0)]),
            (3, 0, [(below, 0)], [(via_1, CH)]),
        ],
    )
    last_1, last_3 = after((late_1, late_3), sums)
    to_3, to_1 = pack([(last_1, 0, 64)], [(last_3, 64, 64)])
    top, bottom = swap(to_3, "y", 3, 4), swap(to_1, "y", 1, 4)
    sums = products(
        ix,
        rows,
        [
            (1, 1, [(late_3, CH)], [(via_3, 0)]),
            (3, 1, [(late_1, CH)], [(via_3, CH)]),
            (2, 0, [(across, 0)], [(late_1, 0)]),
        ],
        sums,
    )
    final = [(2, 1, [(top, 0), (bottom, 0)], [(late_3, 0)])]
    send = products(ix, rows, final, sums, share="send")
    got = swap(send, "c", 1, 2)
    return products(ix, rows, final, sums, share="keep") + got


def solution(mesh):
    fine = Mesh(mesh.devices.reshape(SIZES), AXES)
    return jax.shard_map(
        on_device,
        mesh=fine,
        in_specs=(P(("x", "zl"), ("zh", "y", "c")),),
        out_specs=P(None, ("zh", "y", "c"), ("x", "zl")),
        check_vma=False,
    )
```
